256 devices in a mesh: dev: 256 (over y, z, x, core).
Axes of the slice: x: 4, y: 4, z: 8, core: 2. Of those that a mesh axis runs over, the one named last changes fastest.
Arguments:
- right_sides: bfloat16 [2, 131072, 512], P(None, 'dev'), may hold values from -6 to 6
- factors: bfloat16 [9, 2, 2, 131072, 256], P(None, None, None, 'dev'), may hold values from -0.1875 to 0.1875
Outputs:
- applied: bfloat16 [2, 131072, 512], P(None, 'dev')
The draws below stay inside these ranges and needn't reach their ends.
All inputs are finite; a program needn't handle non-finite values.
Results may differ from the reference program's by a relative error of at most 0.022.
Values may be sent and summed in bfloat16 or wider, within the bound.
No kernel may reach another device: no remote copies, remote signals or barrier semaphores. Data moves between devices by JAX's collectives and lax.ppermute only.
A program may use at most 64 MiB of HBM per device.

```python
import jax
import jax.numpy as jnp

BW = 256
RHS = 512
LEVELS = 9
ORDER = 131072


def block_levels(key, shape, split, least, largest):
    factor_of, own = 1.0, jax.random.fold_in(key, 6)
    for dim, parts in split:
        heights = jnp.exp(jax.random.uniform(jax.random.fold_in(own, dim), (parts,), jnp.float32, least / len(split), largest / len(split)))
        factor_of = factor_of * jnp.repeat(heights, shape[dim] // parts).reshape([-1 if axis == dim else 1 for axis in range(len(shape))])
    return factor_of


def gaussian(own_key, extent, scale, bound, pieces=(), held_as=jnp.bfloat16):
    factor_of = block_levels(own_key, extent, pieces, -0.22, 0.18) if pieces else 1.0
    entries = jax.random.normal(own_key, extent, jnp.float32) * scale * factor_of
    return jnp.minimum(jnp.maximum(entries, -bound), bound).astype(held_as)


def setup_inputs(seed: int = 0) -> dict:
    arg_keys = jax.random.split(jax.random.key(seed), 3)
    return {
        "right_sides": gaussian(arg_keys[0], (2, ORDER, RHS), 1.0, 6.0, ((1, 256),)),
        "factors": gaussian(arg_keys[1], (LEVELS, 2, 2, ORDER, BW), (4 * BW) ** -0.5, 0.1875, ((3, 256),)),
    }


def batched(left, right):
    return jnp.einsum("bic,bcr->bir", left.astype(jnp.float32), right.astype(jnp.float32))


def reference(right_sides, factors):
    nblocks = ORDER // BW
    nbits = nblocks.bit_length() - 1
    field = right_sides.reshape(2, nblocks, BW, RHS)
    for level in range(LEVELS):
        bit = level % nbits
        low = 2 ** bit
        partner = field.reshape(2, nblocks // (2 * low), 2, low, BW, RHS)[:, :, ::-1].reshape(2, nblocks, BW, RHS)
        fac = factors[level].reshape(2, 2, nblocks, BW, BW)
        real_part = batched(fac[0, 0], field[0]) - batched(fac[0, 1], field[1]) + batched(fac[1, 0], partner[0]) - batched(fac[1, 1], partner[1])
        imag_part = batched(fac[0, 0], field[1]) + batched(fac[0, 1], field[0]) + batched(fac[1, 0], partner[1]) + batched(fac[1, 1], partner[0])
        field = jnp.stack([real_part, imag_part]).astype(jnp.bfloat16)
    return field.reshape(2, ORDER, RHS)
```

```python
import jax
import jax.numpy as jnp
from jax import lax
from jax.experimental import pallas as pl
from jax.experimental.pallas import tpu as pltpu
from jax.sharding import PartitionSpec as P

UNIT = 128
STEPS = (
    (0, 1, 2), (0, 6, 8), (0, 4, 6), (1, 1, 2), (0, 2, 4), (1, 4, 5), (1, 7, 8), (0, 0, 1),
    (1, 5, 6), (2, 1, 2), (1, 0, 1), (1, 6, 7), (2, 7, 8), (3, 1, 2), (3, 7, 8), (4, 1, 2),
    (2, 4, 5), (1, 2, 3), (2, 5, 6), (4, 7, 8), (5, 1, 2), (3, 4, 5), (5, 7, 8), (2, 6, 7),
    (4, 4, 5), (3, 5, 6), (1, 3, 4), (6, 1, 2), (5, 4, 5), (4, 5, 6), (3, 6, 7), (2, 3, 4),
    (2, 2, 3), (6, 7, 8), (5, 5, 6), (4, 6, 7), (3, 3, 4), (7, 1, 2), (6, 4, 5), (3, 2, 3),
    (2, 0, 1), (5, 6, 7), (4, 3, 4), (6, 5, 6), (7, 7, 8), (6, 6, 7), (3, 0, 1), (4, 2, 3),
    (5, 3, 4), (8, 1, 2), (7, 5, 6), (7, 6, 7), (4, 0, 1), (5, 2, 3), (7, 4, 5), (6, 3, 4),
    (8, 7, 8), (5, 0, 1), (8, 5, 6), (8, 6, 7), (6, 2, 3), (7, 3, 4), (8, 4, 5), (6, 0, 1),
    (7, 2, 3), (8, 3, 4), (7, 0, 1), (8, 2, 3), (8, 0, 1),
)

VM = pl.BlockSpec(memory_space=pltpu.VMEM)
ANY = pl.BlockSpec(memory_space=pl.ANY)
HBM = pl.BlockSpec(memory_space=pltpu.HBM)


def route(bit):
    return [(i, i ^ (1 << bit)) for i in range(lax.axis_size("dev"))]


def matrix(fac):
    return jnp.concatenate(
        [jnp.concatenate([fac[0, part], fac[1, part]], axis=1) for part in range(2)], axis=0
    )


def butterfly(mat, own, other, out_ref, at):
    w, n = own.shape[1:]
    vec = jnp.concatenate(
        [jnp.concatenate([v[0], v[1]], axis=1) for v in (own, other)], axis=0
    )
    q = jnp.dot(mat, vec, preferred_element_type=jnp.float32)
    out_ref[0, :, at : at + n] = (q[:w, :n] - q[w:, n:]).astype(out_ref.dtype)
    out_ref[1, :, at : at + n] = (q[:w, n:] + q[w:, :n]).astype(out_ref.dtype)


def call(kernel, name, shape, ops, specs, dep, scratch=()):
    if dep is not None:
        ops, specs = ops + [dep], specs + [ANY]
    return pl.pallas_call(
        kernel,
        out_shape=jax.ShapeDtypeStruct(shape, jnp.bfloat16),
        in_specs=specs,
        out_specs=VM,
        scratch_shapes=scratch,
        compiler_params=pltpu.CompilerParams(vmem_limit_bytes=8 << 20),
        cost_estimate=pl.CostEstimate(flops=1, bytes_accessed=1, transcendentals=0),
        name=name,
    )(*ops)


def first_step(b, col, n, sides, factors, dep):
    w = factors.shape[-1]

    def kernel(fac_ref, side_ref, *rest):
        out_ref, fac, vec, sems = rest[-4:]
        at = pl.ds(col, n)
        copies = [
            pltpu.make_async_copy(side_ref.at[:, pl.ds(b * w, w), at], vec.at[0], sems.at[0]),
            pltpu.make_async_copy(side_ref.at[:, pl.ds((1 - b) * w, w), at], vec.at[1], sems.at[1]),
            pltpu.make_async_copy(fac_ref.at[0, :, :, pl.ds(b * w, w)], fac, sems.at[2]),
        ]
        for copy in copies:
            copy.start()
        for copy in copies:
            copy.wait()
        butterfly(matrix(fac[...]), vec[0], vec[1], out_ref, 0)

    scratch = [
        pltpu.VMEM((2, 2, w, w), jnp.bfloat16),
        pltpu.VMEM((2, 2, w, n), jnp.bfloat16),
        pltpu.SemaphoreType.DMA((3,)),
    ]
    return call(kernel, "level0", (2, w, n), [factors, sides], [HBM, HBM], dep, scratch)


def step(level, b, factors, pieces, n, dep):
    w = factors.shape[-1]

    def kernel(fac_ref, *refs):
        out_ref, at = refs[-1], 0
        mat = matrix(fac_ref[level, :, :, pl.ds(b * w, w), :])
        for i, (_, _, low, count) in enumerate(pieces):
            own, other = (ref[:, :, low : low + count] for ref in refs[2 * i : 2 * i + 2])
            butterfly(mat, own, other, out_ref, at)
            at += count

    ops = [factors] + [array for piece in pieces for array in piece[:2]]
    return call(kernel, f"level{level}", (2, w, n), ops, [VM] * len(ops), dep)


def per_device(right_sides, factors):
    levels, w = factors.shape[0], factors.shape[-1]
    rows, sides = right_sides.shape[1:]
    blocks, per_block = rows // w, sides // UNIT
    held = [{} for _ in range(levels)]
    came = [{} for _ in range(levels)]
    dep = None
    for level, first, end in STEPS:
        b, n = first // per_block, (end - first) * UNIT
        if level == 0:
            value = first_step(b, first % per_block * UNIT, n, right_sides, factors, dep)
        else:
            pieces = []
            for group, own in sorted(held[level - 1].items()):
                low, high = max(first, group[0]), min(end, group[1])
                if low < high:
                    if group not in came[level]:
                        came[level][group] = lax.ppermute(own, "dev", route(level - 1))
                    at, count = (low - group[0]) * UNIT, (high - low) * UNIT
                    pieces.append((own, came[level][group], at, count))
            value = step(level, b, factors, pieces, n, dep)
        dep = held[level][first, end] = value
    done = sorted(held[-1].items())
    return jnp.concatenate(
        [
            jnp.concatenate([v for (first, _), v in done if first // per_block == b], axis=2)
            for b in range(blocks)
        ],
        axis=1,
    )


def solution(mesh):
    return jax.shard_map(
        per_device,
        mesh=mesh,
        in_specs=(P(None, "dev", None), P(None, None, None, "dev", None)),
        out_specs=P(None, "dev", None),
        check_vma=False,
    )
```

```python
import jax
import jax.numpy as jnp
from jax import lax
from jax.experimental import pallas as pl
from jax.experimental.pallas import tpu as pltpu
from jax.sharding import PartitionSpec as P

UNIT = 128
STEPS = (
    (0, 1, 2), (1, 1, 2), (0, 6, 8), (0, 4, 6), (0, 2, 4), (1, 4, 5), (1, 7, 8), (0, 0, 1),
    (1, 5, 6), (2, 1, 2), (1, 0, 1), (1, 6, 7), (2, 7, 8), (3, 1, 2), (3, 7, 8), (4, 1, 2),
    (2, 4, 5), (1, 2, 3), (2, 5, 6), (4, 7, 8), (5, 1, 2), (3, 4, 5), (5, 7, 8), (2, 6, 7),
    (4, 4, 5), (3, 5, 6), (1, 3, 4), (6, 1, 2), (5, 4, 5), (4, 5, 6), (3, 6, 7), (2, 3, 4),
    (2, 2, 3), (6, 7, 8), (5, 5, 6), (4, 6, 7), (3, 3, 4), (7, 1, 2), (6, 4, 5), (3, 2, 3),
    (2, 0, 1), (5, 6, 7), (4, 3, 4), (6, 5, 6), (7, 7, 8), (6, 6, 7), (3, 0, 1), (4, 2, 3),
    (5, 3, 4), (8, 1, 2), (7, 5, 6), (7, 6, 7), (4, 0, 1), (5, 2, 3), (7, 4, 5), (6, 3, 4),
    (8, 7, 8), (5, 0, 1), (8, 5, 6), (8, 6, 7), (6, 2, 3), (7, 3, 4), (8, 4, 5), (6, 0, 1),
    (7, 2, 3), (8, 3, 4), (7, 0, 1), (8, 2, 3), (8, 0, 1),
)

VM = pl.BlockSpec(memory_space=pltpu.VMEM)
ANY = pl.BlockSpec(memory_space=pl.ANY)
HBM = pl.BlockSpec(memory_space=pltpu.HBM)


def route(bit):
    return [(i, i ^ (1 << bit)) for i in range(lax.axis_size("dev"))]


def matrix(fac):
    return jnp.concatenate(
        [jnp.concatenate([fac[0, part], fac[1, part]], axis=1) for part in range(2)], axis=0
    )


def butterfly(mat, own, other, out_ref, at):
    w, n = own.shape[1:]
    vec = jnp.concatenate(
        [jnp.concatenate([v[0], v[1]], axis=1) for v in (own, other)], axis=0
    )
    q = jnp.dot(mat, vec, preferred_element_type=jnp.float32)
    out_ref[0, :, at : at + n] = (q[:w, :n] - q[w:, n:]).astype(out_ref.dtype)
    out_ref[1, :, at : at + n] = (q[:w, n:] + q[w:, :n]).astype(out_ref.dtype)


def call(kernel, name, shape, ops, specs, dep, scratch=()):
    if dep is not None:
        ops, specs = ops + [dep], specs + [ANY]
    return pl.pallas_call(
        kernel,
        out_shape=jax.ShapeDtypeStruct(shape, jnp.bfloat16),
        in_specs=specs,
        out_specs=VM,
        scratch_shapes=scratch,
        compiler_params=pltpu.CompilerParams(vmem_limit_bytes=8 << 20),
        cost_estimate=pl.CostEstimate(flops=1, bytes_accessed=1, transcendentals=0),
        name=name,
    )(*ops)


def first_step(b, col, n, sides, factors, dep):
    w = factors.shape[-1]

    def kernel(fac_ref, side_ref, *rest):
        out_ref, fac, vec, sems = rest[-4:]
        at = pl.ds(col, n)
        copies = [
            pltpu.make_async_copy(side_ref.at[:, pl.ds(b * w, w), at], vec.at[0], sems.at[0]),
            pltpu.make_async_copy(side_ref.at[:, pl.ds((1 - b) * w, w), at], vec.at[1], sems.at[1]),
            pltpu.make_async_copy(fac_ref.at[0, :, :, pl.ds(b * w, w)], fac, sems.at[2]),
        ]
        for copy in copies:
            copy.start()
        for copy in copies:
            copy.wait()
        butterfly(matrix(fac[...]), vec[0], vec[1], out_ref, 0)

    scratch = [
        pltpu.VMEM((2, 2, w, w), jnp.bfloat16),
        pltpu.VMEM((2, 2, w, n), jnp.bfloat16),
        pltpu.SemaphoreType.DMA((3,)),
    ]
    return call(kernel, "level0", (2, w, n), [factors, sides], [HBM, HBM], dep, scratch)


def step(level, b, factors, pieces, n, dep):
    w = factors.shape[-1]

    def kernel(fac_ref, *refs):
        out_ref, at = refs[-1], 0
        mat = matrix(fac_ref[level, :, :, pl.ds(b * w, w), :])
        for i, (_, _, low, count) in enumerate(pieces):
            own, other = (ref[:, :, low : low + count] for ref in refs[2 * i : 2 * i + 2])
            butterfly(mat, own, other, out_ref, at)
            at += count

    ops = [factors] + [array for piece in pieces for array in piece[:2]]
    return call(kernel, f"level{level}", (2, w, n), ops, [VM] * len(ops), dep)


def per_device(right_sides, factors):
    levels, w = factors.shape[0], factors.shape[-1]
    rows, sides = right_sides.shape[1:]
    blocks, per_block = rows // w, sides // UNIT
    held = [{} for _ in range(levels)]
    came = [{} for _ in range(levels)]
    dep = None
    for level, first, end in STEPS:
        b, n = first // per_block, (end - first) * UNIT
        if level == 0:
            value = first_step(b, first % per_block * UNIT, n, right_sides, factors, dep)
        else:
            pieces = []
            for group, own in sorted(held[level - 1].items()):
                low, high = max(first, group[0]), min(end, group[1])
                if low < high:
                    if group not in came[level]:
                        came[level][group] = lax.ppermute(own, "dev", route(level - 1))
                    at, count = (low - group[0]) * UNIT, (high - low) * UNIT
                    pieces.append((own, came[level][group], at, count))
            value = step(level, b, factors, pieces, n, dep)
        dep = held[level][first, end] = value
    done = sorted(held[-1].items())
    return jnp.concatenate(
        [
            jnp.concatenate([v for (first, _), v in done if first // per_block == b], axis=2)
            for b in range(blocks)
        ],
        axis=1,
    )


def solution(mesh):
    return jax.shard_map(
        per_device,
        mesh=mesh,
        in_specs=(P(None, "dev", None), P(None, None, None, "dev", None)),
        out_specs=P(None, "dev", None),
        check_vma=False,
    )
```
